256 devices in a mesh: grid: 8 (over y, core), mesh: 32 (over x, z).
Axes of the slice: x: 4, y: 4, z: 8, core: 2. Of those that a mesh axis runs over, the one named last changes fastest.
Arguments:
- grid_feats: bfloat16 [131072, 227], P(('grid', 'mesh')), may hold values from -6 to 6
- g2m_src: int32 [768, 256], P(('grid', 'mesh')), may hold values from 0 to 511
- g2m_count: int32 [256, 3], P(('grid', 'mesh')), may hold values from 32 to 256, as said below
- g2m_dst: int32 [768, 256], P(('grid', 'mesh')), may hold values from 0 to 63
- g2m_weight: bfloat16 [768, 256], P(('grid', 'mesh')), may hold values from 0.29882812 to 3
- halo_send: int32 [8192, 16], P(('grid', 'mesh')), may hold values from 0 to 63
- mesh_src: int32 [16384, 6], P(('grid', 'mesh')), may hold values from 0 to 575
- cotangent: bfloat16 [16384, 512], P(('grid', 'mesh')), may hold values from -24 to 24
- w_embed: bfloat16 [227, 512], replicated, may hold values from -0.375 to 0.375
- w_encode: bfloat16 [2, 512, 512], replicated, may hold values from -0.25 to 0.25
- w_layers: bfloat16 [2, 3, 512, 512], replicated, may hold values from -0.25 to 0.25
- gains: float32 [4, 512], replicated, may hold values from 0.5 to 1.5
Outputs:
- mesh_out: bfloat16 [16384, 512], P(('grid', 'mesh'))
- grad_layers: float32 [2, 3, 512, 512], P(None, None, None, 'mesh')
- grad_encoder: float32 [2, 512, 512], P(None, None, 'mesh')
- grad_embed: float32 [227, 512], replicated
The draws below stay inside these ranges and needn't reach their ends.
Inputs may be any that keep to these rules, and one draw needn't show every extreme that they name: `g2m_count`: multiples of 32; slots are used from slot 0 on; in every band some sector receives all 256 slots from each of its three sources. `mesh_src`: rows below 64 are the sector's own nodes; row 64 + m * 16 + k is the k-th row copied from sector m of the band.
All inputs are finite; a program needn't handle non-finite values.
Results may differ from the reference program's by a relative error of at most 0.03.
Values may be sent and summed in bfloat16 or wider, within the bound.
No kernel may reach another device: no remote copies, remote signals or barrier semaphores. Data moves between devices by JAX's collectives and lax.ppermute only.
A program may use at most 128 MiB of HBM per device.

```python
import math
import jax
import jax.numpy as jnp
from jax import lax

WIDTH = 512
CHANNELS = 227
GRID_DEV = 512
NODE_DEV = 64
HALO_ROWS = 16
DEGREE = 6
LAYERS = 2
ROW_BLOCK = 32
SLOTS = 256
GRID_NODES = 131072
MESH_NODES = 16384
EDGE_BLOCKS = 768
PAIR_BLOCKS = 8192
N_GRID = 8
N_MESH = 32


def draw_g2m_count(key, part):
    key = jax.random.fold_in(key, 7)
    key_own, key_side, key_full = jax.random.split(key, 3)
    own_count = jax.random.randint(key_own, (N_GRID, N_MESH, 1), 4, 9) * ROW_BLOCK
    side_count = jax.random.randint(key_side, (N_GRID, N_MESH, 3), 1, 5) * ROW_BLOCK
    offset = jnp.arange(3)[None, None, :]
    sector = jnp.arange(N_MESH)[None, :, None]
    counts = jnp.where(offset == 1, own_count, side_count)
    chosen = jax.random.randint(key_full, (N_GRID, 1, 1), 0, N_MESH)
    full_own = (sector == chosen) & (offset == 1)
    full_west = (sector == (chosen + N_MESH - 1) % N_MESH) & (offset == 2)
    full_east = (sector == (chosen + 1) % N_MESH) & (offset == 0)
    counts = jnp.where(full_own | full_west | full_east, SLOTS, counts)
    return counts.reshape(N_GRID * N_MESH, 3).astype(jnp.int32)


def with_ends(entries, rng, least, top_value):
    dims = entries.shape
    index_at = [jax.random.randint(jax.random.fold_in(rng, axis), (), 0, dims[axis]) for axis in range(len(dims))]
    entries = entries.at[tuple(index_at)].set(least)
    longest = dims.index(max(dims))
    index_at[longest] = (index_at[longest] + 1) % dims[longest]
    return entries.at[tuple(index_at)].set(top_value)


def with_spikes(entries, own_key, source, target, blocks, factor):
    owner, partner = [(jnp.arange(entries.shape[dim]) // (entries.shape[dim] // blocks)).reshape([-1 if axis == dim else 1 for axis in range(entries.ndim)]) for dim in (source, target)]
    chosen = jax.random.permutation(own_key, blocks)[partner]
    strong = (owner == chosen) | (owner == (partner + blocks // 2) % blocks)
    return jnp.where(strong, factor * entries, entries)


def block_levels(stream_key, dims, cuts, low, largest):
    def one(dim, blocks):
        steps = jax.random.uniform(jax.random.fold_in(jax.random.fold_in(stream_key, 6), dim), (blocks,), jnp.float32, low / len(cuts), largest / len(cuts))
        return jnp.repeat(jnp.exp(steps), dims[dim] // blocks).reshape((-1,) + (1,) * (len(dims) - dim - 1))

    loudness = one(*cuts[0])
    for cut in cuts[1:]:
        loudness = loudness * one(*cut)
    return loudness


def normal_values(key, shape, deviation, most, cuts=(), dtype=jnp.bfloat16):
    level = block_levels(key, shape, cuts, -0.22, 0.18) if cuts else 1.0
    result = jax.random.normal(key, shape, jnp.float32) * deviation * level
    return jnp.minimum(jnp.maximum(result, -most), most).astype(dtype)


def bell_draw_with(key, dims, spread, limit, cuts, heavy, held_as=jnp.bfloat16):
    drawn = spread * jax.random.normal(key, dims, jnp.float32)
    if cuts:
        drawn = drawn * block_levels(key, dims, cuts, -0.22, 0.18)
    return jnp.clip(with_spikes(drawn, jax.random.fold_in(key, 3), *heavy), -limit, limit).astype(held_as)


def setup_inputs(seed: int = 0) -> dict:
    key_list = jax.random.split(jax.random.key(seed), 13)
    return {
        "grid_feats": normal_values(key_list[0], (GRID_NODES, CHANNELS), 1.0, 6.0, ((0, 256),)),
        "g2m_src": with_ends(jax.random.randint(key_list[1], (EDGE_BLOCKS, SLOTS), 0, GRID_DEV), jax.random.fold_in(key_list[1], 1), 0, GRID_DEV - 1).astype(jnp.int32),
        "g2m_count": draw_g2m_count(jax.random.fold_in(key_list[12], 71), 0),
        "g2m_dst": with_ends(jax.random.randint(key_list[3], (EDGE_BLOCKS, SLOTS), 0, NODE_DEV), jax.random.fold_in(key_list[3], 1), 0, NODE_DEV - 1).astype(jnp.int32),
        "g2m_weight": jnp.clip(jnp.exp(math.log(3.0) - 2.306499 * jax.random.uniform(key_list[4], (EDGE_BLOCKS, SLOTS), jnp.float32) ** block_levels(key_list[4], (EDGE_BLOCKS, SLOTS), ((0, 256),), -0.2, 0.2)), 0.29882812, 3.0).astype(jnp.bfloat16),
        "halo_send": with_ends(jax.random.randint(key_list[5], (PAIR_BLOCKS, HALO_ROWS), 0, NODE_DEV), jax.random.fold_in(key_list[5], 1), 0, NODE_DEV - 1).astype(jnp.int32),
        "mesh_src": with_ends(jax.random.randint(key_list[6], (MESH_NODES, DEGREE), 0, NODE_DEV + N_MESH * HALO_ROWS), jax.random.fold_in(key_list[6], 1), 0, (NODE_DEV + N_MESH * HALO_ROWS) - 1).astype(jnp.int32),
        "cotangent": bell_draw_with(key_list[7], (MESH_NODES, WIDTH), 1.0, 24.0, ((0, 256),), (0, 1, 256, 6.0)),
        "w_embed": normal_values(key_list[8], (CHANNELS, WIDTH), CHANNELS ** -0.5, 0.375),
        "w_encode": normal_values(key_list[9], (2, WIDTH, WIDTH), WIDTH ** -0.5, 0.25),
        "w_layers": normal_values(key_list[10], (LAYERS, 3, WIDTH, WIDTH), WIDTH ** -0.5, 0.25),
        "gains": jnp.clip(jax.random.uniform(key_list[11], (2 + LAYERS, WIDTH), jnp.float32, 0.5, 1.5), 0.5, 1.5),
    }


NORM_EPSILON = 1e-05

def normalize(values):
    average = lax.optimization_barrier(jnp.mean(values, axis=-1, keepdims=True))
    centred = values - average
    inverse = lax.rsqrt(lax.optimization_barrier(jnp.mean(centred * centred, axis=-1, keepdims=True)) + NORM_EPSILON)
    return (centred * inverse, inverse)

def normalize_back(grad_hat, normed, inverse):
    first = lax.optimization_barrier(jnp.mean(grad_hat, axis=-1, keepdims=True))
    second = lax.optimization_barrier(jnp.mean(grad_hat * normed, axis=-1, keepdims=True))
    return inverse * (grad_hat - first - normed * second)

def silu_slope(values):
    logistic = jax.nn.sigmoid(values)
    return logistic * (1.0 + values * (1.0 - logistic))

def matmul(matrix_a, matrix_b):
    return jnp.dot(matrix_a, matrix_b, preferred_element_type=jnp.float32)

def outer_total(pattern, matrix_a, matrix_b):
    return jnp.einsum(pattern, matrix_a.astype(jnp.float32), matrix_b.astype(jnp.float32), precision=lax.Precision.HIGHEST)

def take_rows(source_rows, index_rows):
    return source_rows[index_rows]

def scatter_rows(value_rows, index_rows, segments):
    feature_width = value_rows.shape[-1]
    return jax.ops.segment_sum(value_rows.reshape(-1, feature_width), index_rows.reshape(-1), num_segments=segments)

def across_sides(blocks):
    return jnp.stack([jnp.roll(blocks[:, 2 - side], 1 - side, axis=0) for side in range(3)], axis=1)

def band_pass(band_data, w_embed, w_encode, w_layers, gains):
    features, sources, counts, targets, weights, sends, links, cotan = band_data
    peer_count = sources.shape[0]
    slot_count = sources.shape[2]
    halo_count = sends.shape[2]
    node_count = links.shape[1]
    grid_count = features.shape[1]
    feature_width = w_embed.shape[1]
    grid_pre = matmul(features, w_embed)
    normed_grid, inverse_grid = normalize(jax.nn.silu(grid_pre))
    grid_latent = (normed_grid * gains[0]).astype(jnp.bfloat16)
    live_slots = jnp.arange(slot_count)[None, None, :] < counts[:, :, None]
    picked = jax.vmap(take_rows)(grid_latent, sources)
    edge_rows = jnp.where(live_slots[..., None], picked, jnp.zeros((), jnp.bfloat16))
    edge_pre = matmul(edge_rows, w_encode[0])
    edge_message = jax.nn.silu(edge_pre).astype(jnp.bfloat16)
    received = across_sides(edge_message)
    onehot = jnp.where(targets[:, None, :, :] == jnp.arange(node_count)[None, :, None, None], weights[:, None, :, :], jnp.zeros((), jnp.bfloat16))
    mesh_sum = outer_total('bnsj,bsjd->bnd', onehot, received).astype(jnp.bfloat16)
    normed_start, inverse_start = normalize(matmul(mesh_sum, w_encode[1]))
    latent = (normed_start * gains[1]).astype(jnp.bfloat16)
    stored = []
    for layer_index in range(LAYERS):
        sent_rows = jax.vmap(take_rows)(latent, sends)
        halo_latent = jnp.swapaxes(sent_rows, 0, 1).reshape(peer_count, peer_count * halo_count, feature_width)
        node_table = jnp.concatenate([latent, halo_latent], axis=1)
        gathered = jax.vmap(take_rows)(node_table, links)
        pair_pre = matmul(gathered, w_layers[layer_index, 0]) + matmul(latent, w_layers[layer_index, 1])[:, :, None, :]
        pair_message = jax.nn.silu(pair_pre).astype(jnp.bfloat16)
        node_sum = lax.optimization_barrier(jnp.sum(pair_message.astype(jnp.float32), axis=2)).astype(jnp.bfloat16)
        normed, inverse = normalize(matmul(node_sum, w_layers[layer_index, 2]))
        stored.append((latent, gathered, pair_pre, node_sum, normed, inverse))
        latent = (latent.astype(jnp.float32) + normed * gains[2 + layer_index]).astype(jnp.bfloat16)
    mesh_out = latent
    loss_scale = 1.0 / math.sqrt(NODE_DEV * N_GRID * N_MESH)
    upstream = cotan.astype(jnp.float32) * loss_scale
    layer_grads = []
    for layer_index in reversed(range(LAYERS)):
        latent_in, gathered, pair_pre, node_sum, normed, inverse = stored[layer_index]
        grad_norm = normalize_back(upstream * gains[2 + layer_index], normed, inverse).astype(jnp.bfloat16)
        grad_out = outer_total('bnd,bne->de', node_sum, grad_norm)
        grad_node = matmul(grad_norm, w_layers[layer_index, 2].T)
        grad_pair_pre = grad_node[:, :, None, :] * silu_slope(pair_pre)
        grad_pair = grad_pair_pre.astype(jnp.bfloat16)
        grad_self = lax.optimization_barrier(jnp.sum(grad_pair_pre, axis=2)).astype(jnp.bfloat16)
        grad_far = outer_total('bnkd,bnke->de', gathered, grad_pair)
        grad_near = outer_total('bnd,bne->de', latent_in, grad_self)
        grad_rows = matmul(grad_pair, w_layers[layer_index, 0].T)
        table_rows = node_count + peer_count * halo_count
        grad_table = jax.vmap(lambda value_rows, index_rows: scatter_rows(value_rows, index_rows, table_rows))(grad_rows, links)
        returned_grads = jnp.swapaxes(grad_table[:, node_count:].reshape(peer_count, peer_count, halo_count, feature_width), 0, 1)
        copied = jax.vmap(lambda value_rows, index_rows: scatter_rows(value_rows, index_rows, node_count))(returned_grads, sends)
        upstream = upstream + matmul(grad_self, w_layers[layer_index, 1].T) + grad_table[:, :node_count] + copied
        layer_grads.insert(0, jnp.stack([grad_far, grad_near, grad_out]))
    grad_start = normalize_back(upstream * gains[1], normed_start, inverse_start).astype(jnp.bfloat16)
    grad_node_w = outer_total('bnd,bne->de', mesh_sum, grad_start)
    grad_mesh_sum = matmul(grad_start, w_encode[1].T).astype(jnp.bfloat16)
    picked_grads = jax.vmap(take_rows)(grad_mesh_sum, targets)
    grad_message = (weights.astype(jnp.float32)[..., None] * picked_grads.astype(jnp.float32)).astype(jnp.bfloat16)
    returned_message = across_sides(grad_message)
    grad_edge = (returned_message.astype(jnp.float32) * silu_slope(edge_pre)).astype(jnp.bfloat16)
    grad_edge_w = outer_total('bojd,boje->de', edge_rows, grad_edge)
    grad_sent = matmul(grad_edge, w_encode[0].T)
    grad_sent = jnp.where(live_slots[..., None], grad_sent, jnp.zeros((), jnp.float32))
    grad_grid = jax.vmap(lambda value_rows, index_rows: scatter_rows(value_rows, index_rows, grid_count))(grad_sent, sources)
    grad_act = (normalize_back(grad_grid * gains[0], normed_grid, inverse_grid) * silu_slope(grid_pre)).astype(jnp.bfloat16)
    grad_embed = outer_total('bgc,bgd->cd', features, grad_act)
    return (mesh_out, jnp.stack(layer_grads), jnp.stack([grad_edge_w, grad_node_w]), grad_embed)

def reference(grid_feats, g2m_src, g2m_count, g2m_dst, g2m_weight, halo_send, mesh_src, cotangent, w_embed, w_encode, w_layers, gains):
    band_data = (grid_feats.reshape(N_GRID, N_MESH, GRID_DEV, CHANNELS), g2m_src.reshape(N_GRID, N_MESH, 3, SLOTS), g2m_count.reshape(N_GRID, N_MESH, 3), g2m_dst.reshape(N_GRID, N_MESH, 3, SLOTS), g2m_weight.reshape(N_GRID, N_MESH, 3, SLOTS), halo_send.reshape(N_GRID, N_MESH, N_MESH, HALO_ROWS), mesh_src.reshape(N_GRID, N_MESH, NODE_DEV, DEGREE), cotangent.reshape(N_GRID, N_MESH, NODE_DEV, WIDTH))
    results = lax.map(lambda single: band_pass(single, w_embed, w_encode, w_layers, gains), band_data)
    mesh_out = results[0].reshape(N_GRID * N_MESH * NODE_DEV, WIDTH)
    return (mesh_out, lax.optimization_barrier(jnp.sum(results[1], axis=0)), lax.optimization_barrier(jnp.sum(results[2], axis=0)), lax.optimization_barrier(jnp.sum(results[3], axis=0)))
```

```python
import math

import jax
import jax.numpy as jnp
from jax import lax
from jax.sharding import PartitionSpec as P

NORM_EPSILON = 1e-05


def side_pairs(count):
    forward = [(i, (i + 1) % count) for i in range(count)]
    backward = [((i + 1) % count, i) for i in range(count)]
    return forward, backward


def from_sides(to_east, to_west):
    forward, backward = side_pairs(lax.axis_size("mesh"))
    return lax.ppermute(to_east, "mesh", forward), lax.ppermute(to_west, "mesh", backward)


def exchange(blocks, axis):
    return lax.all_to_all(blocks, axis, split_axis=0, concat_axis=0, tiled=True)


def spread(block, axis):
    count = lax.axis_size(axis)
    return exchange(jnp.broadcast_to(block[None], (count,) + block.shape), axis)


def over_grid(grads):
    count = lax.axis_size("grid")
    stack, rows, width = grads.shape
    ordered = grads.reshape(stack, count, rows // count, width).transpose(1, 0, 2, 3)
    return lax.psum_scatter(
        ordered.reshape(-1, width), "grid", scatter_dimension=0, tiled=True
    )


def normalize(values):
    average = jnp.mean(values, axis=-1, keepdims=True)
    centred = values - average
    inverse = lax.rsqrt(jnp.mean(centred * centred, axis=-1, keepdims=True) + NORM_EPSILON)
    return (centred * inverse, inverse)


def normalize_back(grad_hat, normed, inverse):
    first = jnp.mean(grad_hat, axis=-1, keepdims=True)
    second = jnp.mean(grad_hat * normed, axis=-1, keepdims=True)
    return inverse * (grad_hat - first - normed * second)


def silu_slope(values):
    logistic = jax.nn.sigmoid(values)
    return logistic * (1.0 + values * (1.0 - logistic))


def matmul(matrix_a, matrix_b):
    return jnp.dot(matrix_a, matrix_b, preferred_element_type=jnp.float32)


def left_transposed(matrix_a, matrix_b):
    return lax.dot_general(
        matrix_a, matrix_b, (((0,), (0,)), ((), ())), preferred_element_type=jnp.float32
    )


def right_transposed(matrix_a, matrix_b):
    return lax.dot_general(
        matrix_a, matrix_b, (((1,), (1,)), ((), ())), preferred_element_type=jnp.float32
    )


def local(
    grid_feats,
    g2m_src,
    g2m_count,
    g2m_dst,
    g2m_weight,
    halo_send,
    mesh_src,
    cotangent,
    w_embed,
    w_encode,
    w_layers,
    gains,
):
    peer_count = lax.axis_size("mesh")
    node_count = mesh_src.shape[0]
    feature_width = w_embed.shape[1]
    slot_count = g2m_src.shape[1]
    halo_count = halo_send.shape[1]
    layer_count = w_layers.shape[0]
    grid_count = lax.axis_size("grid")
    channel_count = grid_feats.shape[1]
    columns = feature_width // peer_count
    edge_info = jnp.stack([g2m_dst.astype(jnp.float32), g2m_weight.astype(jnp.float32)], axis=1)
    info_west, info_east = from_sides(edge_info[2], edge_info[0])
    target_info = jnp.stack([info_west, edge_info[1], info_east])
    grid_pre = matmul(grid_feats, w_embed)
    normed_grid, inverse_grid = normalize(jax.nn.silu(grid_pre))
    grid_latent = (normed_grid * gains[0]).astype(jnp.bfloat16)
    live_slots = jnp.arange(slot_count)[None, :] < g2m_count[0][:, None]
    edge_rows = jnp.where(live_slots[:, :, None], grid_latent[g2m_src], jnp.zeros((), jnp.bfloat16))
    edge_pre = matmul(edge_rows, w_encode[0])
    edge_message = jax.nn.silu(edge_pre).astype(jnp.bfloat16)
    onehot = jnp.where(
        target_info[:, 0, None, :] == jnp.arange(node_count, dtype=jnp.float32)[None, :, None],
        target_info[:, 1, None, :],
        0.0,
    ).astype(jnp.bfloat16)
    partial_sums = jnp.einsum(
        "onj,ojd->ond", onehot, edge_message, preferred_element_type=jnp.float32
    )
    sent_sums = partial_sums.astype(jnp.bfloat16)
    sum_west, sum_east = from_sides(sent_sums[2], sent_sums[0])
    mesh_sum = (
        partial_sums[1] + sum_west.astype(jnp.float32) + sum_east.astype(jnp.float32)
    ).astype(jnp.bfloat16)
    normed_start, inverse_start = normalize(matmul(mesh_sum, w_encode[1]))
    latent = (normed_start * gains[1]).astype(jnp.bfloat16)
    stored = []
    for layer_index in range(layer_count):
        halo_latent = lax.all_to_all(
            latent[halo_send], "mesh", split_axis=0, concat_axis=0, tiled=True
        ).reshape(-1, feature_width)
        node_table = jnp.concatenate([latent, halo_latent], axis=0)
        gathered = node_table[mesh_src]
        pair_pre = (
            matmul(gathered, w_layers[layer_index, 0])
            + matmul(latent, w_layers[layer_index, 1])[:, None, :]
        )
        pair_message = jax.nn.silu(pair_pre).astype(jnp.bfloat16)
        node_sum = jnp.sum(pair_message.astype(jnp.float32), axis=1).astype(jnp.bfloat16)
        normed, inverse = normalize(matmul(node_sum, w_layers[layer_index, 2]))
        stored.append((latent, gathered, pair_pre, node_sum, normed, inverse))
        latent = (latent.astype(jnp.float32) + normed * gains[2 + layer_index]).astype(jnp.bfloat16)
    loss_scale = 1.0 / math.sqrt(node_count * lax.axis_size("grid") * peer_count)
    upstream = cotangent.astype(jnp.float32) * loss_scale
    layer_grads = []
    reduced = []
    for layer_index in reversed(range(layer_count)):
        latent_in, gathered, pair_pre, node_sum, normed, inverse = stored[layer_index]
        grad_norm = normalize_back(upstream * gains[2 + layer_index], normed, inverse).astype(
            jnp.bfloat16
        )
        grad_out = left_transposed(node_sum, grad_norm)
        grad_node = right_transposed(grad_norm, w_layers[layer_index, 2])
        grad_pair_pre = grad_node[:, None, :] * silu_slope(pair_pre)
        grad_pair = grad_pair_pre.astype(jnp.bfloat16).reshape(-1, feature_width)
        grad_self = jnp.sum(grad_pair_pre, axis=1).astype(jnp.bfloat16)
        grad_far = left_transposed(gathered.reshape(-1, feature_width), grad_pair)
        grad_near = left_transposed(latent_in, grad_self)
        grad_rows = right_transposed(grad_pair, w_layers[layer_index, 0])
        grad_table = jax.ops.segment_sum(
            grad_rows, mesh_src.reshape(-1), num_segments=node_count + peer_count * halo_count
        )
        returned_grads = lax.all_to_all(
            grad_table[node_count:]
            .reshape(peer_count, halo_count, feature_width)
            .astype(jnp.bfloat16),
            "mesh",
            split_axis=0,
            concat_axis=0,
            tiled=True,
        ).astype(jnp.float32)
        copied = jax.ops.segment_sum(
            returned_grads.reshape(-1, feature_width),
            halo_send.reshape(-1),
            num_segments=node_count,
        )
        upstream = (
            upstream
            + right_transposed(grad_self, w_layers[layer_index, 1])
            + grad_table[:node_count]
            + copied
        )
        layer_grads.insert(0, jnp.stack([grad_far, grad_near, grad_out]).astype(jnp.bfloat16))
        if layer_index > 0:
            reduced.append(over_grid(layer_grads[0]))
    grad_start = normalize_back(upstream * gains[1], normed_start, inverse_start).astype(
        jnp.bfloat16
    )
    grad_node_w = left_transposed(mesh_sum, grad_start)
    grad_mesh_sum = right_transposed(grad_start, w_encode[1]).astype(jnp.bfloat16)
    reduced.append(
        over_grid(jnp.concatenate([layer_grads[0], grad_node_w.astype(jnp.bfloat16)[None]]))
    )
    split = jnp.concatenate(reduced).T.reshape(peer_count, columns, -1)
    shared_sums = jnp.sum(exchange(split, "mesh").astype(jnp.float32), axis=0)
    west_grads, east_grads = from_sides(grad_mesh_sum, grad_mesh_sum)
    grad_targets = jnp.stack([west_grads, grad_mesh_sum, east_grads])
    grad_message = jnp.einsum(
        "onj,ond->ojd", onehot, grad_targets, preferred_element_type=jnp.float32
    ).astype(jnp.bfloat16)
    grad_edge = (
        (grad_message.astype(jnp.float32) * silu_slope(edge_pre))
        .astype(jnp.bfloat16)
        .reshape(-1, feature_width)
    )
    grad_sent = right_transposed(grad_edge, w_encode[0]).reshape(3, slot_count, feature_width)
    grad_sent = jnp.where(live_slots[:, :, None], grad_sent, jnp.zeros((), jnp.float32))
    grad_grid = jax.ops.segment_sum(
        grad_sent.reshape(-1, feature_width), g2m_src.reshape(-1), num_segments=grid_feats.shape[0]
    )
    grad_act = (
        normalize_back(grad_grid * gains[0], normed_grid, inverse_grid) * silu_slope(grid_pre)
    ).astype(jnp.bfloat16)
    padded = jnp.pad(grid_feats, ((0, 0), (0, -channel_count % 128)))
    last = jnp.concatenate(
        [
            left_transposed(grad_edge, edge_rows.reshape(-1, feature_width)),
            left_transposed(grad_act, padded),
        ],
        axis=1,
    ).astype(jnp.bfloat16)
    last = exchange(last.reshape(peer_count, columns, -1), "mesh")
    last_sums = jnp.sum(last.astype(jnp.float32), axis=0)
    held = jnp.concatenate([shared_sums, last_sums], axis=1).astype(jnp.bfloat16)
    held = spread(held, "grid")
    shared_count = shared_sums.shape[1]
    whole = held[:, :, :shared_count].reshape(grid_count, columns, -1, feature_width // grid_count)
    whole = whole.transpose(2, 0, 3, 1).reshape(-1, feature_width, columns).astype(jnp.float32)
    last_sums = jnp.sum(held[:, :, shared_count:].astype(jnp.float32), axis=0)
    grad_edge_w = last_sums[:, :feature_width].T
    embed = spread(last_sums[:, feature_width:].astype(jnp.bfloat16), "mesh")
    total_embed = embed.reshape(feature_width, -1).T[:channel_count].astype(jnp.float32)
    return (
        latent,
        jnp.concatenate([whole[3:6], whole[:3]]).reshape(layer_count, 3, feature_width, columns),
        jnp.stack([grad_edge_w, whole[6]]),
        total_embed,
    )


def solution(mesh):
    placed = (
        P(("grid", "mesh"), None),
        P(("grid", "mesh"), None),
        P(("grid", "mesh"), None),
        P(("grid", "mesh"), None),
        P(("grid", "mesh"), None),
        P(("grid", "mesh"), None),
        P(("grid", "mesh"), None),
        P(("grid", "mesh"), None),
        P(),
        P(),
        P(),
        P(),
    )
    return jax.shard_map(
        local,
        mesh=mesh,
        in_specs=placed,
        out_specs=(
            P(("grid", "mesh"), None),
            P(None, None, None, "mesh"),
            P(None, None, "mesh"),
            P(),
        ),
        check_vma=False,
    )
```

```python
import math

import jax
import jax.numpy as jnp
from jax import lax
from jax.experimental import pallas as pl
from jax.experimental.pallas import tpu as pltpu
from jax.sharding import PartitionSpec as P

NORM_EPSILON = 1e-05
BF16 = jnp.bfloat16
F32 = jnp.float32


def side_pairs(count):
    forward = [(i, (i + 1) % count) for i in range(count)]
    backward = [((i + 1) % count, i) for i in range(count)]
    return forward, backward


def from_sides(to_east, to_west):
    forward, backward = side_pairs(lax.axis_size("mesh"))
    return lax.ppermute(to_east, "mesh", forward), lax.ppermute(to_west, "mesh", backward)


def exchange(blocks, axis):
    return lax.all_to_all(blocks, axis, split_axis=0, concat_axis=0, tiled=True)


def spread(block, axis):
    count = lax.axis_size(axis)
    return exchange(jnp.broadcast_to(block[None], (count,) + block.shape), axis)


def along_y(block, step):
    count = lax.axis_size("grid")
    return lax.ppermute(block, "grid", [(i, (i + 2 * step) % count) for i in range(count)])


def to_other_core(block):
    return lax.ppermute(block, "grid", [(i, i ^ 1) for i in range(lax.axis_size("grid"))])


def normalize(values):
    average = jnp.mean(values, axis=-1, keepdims=True)
    centred = values - average
    inverse = lax.rsqrt(jnp.mean(centred * centred, axis=-1, keepdims=True) + NORM_EPSILON)
    return (centred * inverse, inverse)


def normalize_back(grad_hat, normed, inverse):
    first = jnp.mean(grad_hat, axis=-1, keepdims=True)
    second = jnp.mean(grad_hat * normed, axis=-1, keepdims=True)
    return inverse * (grad_hat - first - normed * second)


def silu(values):
    return values * jax.nn.sigmoid(values)


def silu_slope(values):
    logistic = jax.nn.sigmoid(values)
    return logistic * (1.0 + values * (1.0 - logistic))


def matmul(matrix_a, matrix_b):
    return jnp.dot(matrix_a, matrix_b, preferred_element_type=F32)


def left_transposed(matrix_a, matrix_b):
    return lax.dot_general(
        matrix_a, matrix_b, (((0,), (0,)), ((), ())), preferred_element_type=F32
    )


def right_transposed(matrix_a, matrix_b):
    return lax.dot_general(
        matrix_a, matrix_b, (((1,), (1,)), ((), ())), preferred_element_type=F32
    )


def hits(index_row, count):
    rows = lax.broadcasted_iota(jnp.int32, (count, index_row.shape[1]), 0)
    return jnp.where(rows == index_row, 1.0, 0.0).astype(BF16)


def weighted_hits(info, count):
    rows = lax.broadcasted_iota(jnp.int32, (count, info.shape[1]), 0).astype(F32)
    return jnp.where(rows == info[0:1], info[1:2], 0.0).astype(BF16)


def live_hits(index_row, live, count):
    shape = (count, index_row.shape[1])
    rows = lax.broadcasted_iota(jnp.int32, shape, 0)
    slots = lax.broadcasted_iota(jnp.int32, shape, 1)
    return jnp.where((rows == index_row) & (slots < live), 1.0, 0.0).astype(BF16)


def call(kernel, outs, args, flops, scalars=(), picked=None):
    picked = picked or {}
    specs = []
    for place, arg in enumerate(args):
        if place in scalars:
            specs.append(pl.BlockSpec(memory_space=pltpu.SMEM))
        elif place in picked:
            lead, zeros = picked[place], (0,) * (arg.ndim - 1)
            specs.append(
                pl.BlockSpec((None,) + arg.shape[1:], lambda i, lead=lead, zeros=zeros: (lead,) + zeros)
            )
        else:
            specs.append(pl.BlockSpec(arg.shape, lambda i, zeros=(0,) * arg.ndim: zeros))
    shapes = [jax.ShapeDtypeStruct(shape, dtype) for shape, dtype in outs]
    moved = sum(math.prod(s.shape) * s.dtype.itemsize for s in list(args) + shapes)
    return pl.pallas_call(
        kernel,
        grid=(1,),
        in_specs=specs,
        out_specs=[
            pl.BlockSpec(s.shape, lambda i, zeros=(0,) * len(s.shape): zeros) for s in shapes
        ],
        out_shape=shapes,
        compiler_params=pltpu.CompilerParams(vmem_limit_bytes=60 * 2**20),
        cost_estimate=pl.CostEstimate(flops=flops, bytes_accessed=moved, transcendentals=0),
    )(*args)


def edge_forward(counts, feats, sources, w_embed, w_edge, gains, pre_out, rows_out, edge_out, message_out):
    grid_pre = left_transposed(feats[...], w_embed[...])
    pre_out[...] = grid_pre
    normed, _ = normalize(silu(grid_pre))
    latent = (normed * gains[0:1]).astype(BF16)
    slots = sources.shape[1]
    for side in range(3):
        chosen = live_hits(sources[side : side + 1], counts[0, side], latent.shape[0])
        rows = left_transposed(chosen, latent).astype(BF16)
        edge_pre = matmul(rows, w_edge[...])
        place = pl.ds(side * slots, slots)
        rows_out[place] = rows
        edge_out[place] = edge_pre
        message_out[place] = silu(edge_pre).astype(BF16)


def edge_sums(info_west, info_own, info_east, messages, west_out, own_out, east_out):
    nodes = own_out.shape[0]
    slots = info_own.shape[1]
    sides = ((info_west, west_out), (info_own, own_out), (info_east, east_out))
    for side, (info, out) in enumerate(sides):
        total = matmul(weighted_hits(info[...], nodes), messages[pl.ds(side * slots, slots)])
        out[...] = total.astype(out.dtype)


def mesh_start(own, west, east, w_node, gains, sends, sum_out, latent_out, sent_out):
    mesh_sum = (own[...] + west[...].astype(F32) + east[...].astype(F32)).astype(BF16)
    sum_out[...] = mesh_sum
    normed, _ = normalize(matmul(mesh_sum, w_node[...]))
    latent = (normed * gains[1:2]).astype(BF16)
    latent_out[...] = latent
    sent_out[...] = left_transposed(hits(sends[...], latent.shape[0]), latent).astype(BF16)


def layer_values(latent, halo, links, weights, degree):
    nodes, width = latent.shape
    own = left_transposed(hits(links, nodes), latent)
    far = left_transposed(hits(links - nodes, halo.shape[0]), halo)
    gathered = (own + far).astype(BF16)
    pair_pre = matmul(gathered, weights[0]).reshape(degree, nodes, width) + matmul(latent, weights[1])[None]
    message = silu(pair_pre).astype(BF16)
    node_sum = jnp.sum(message.astype(F32), axis=0).astype(BF16)
    return gathered, pair_pre, node_sum, matmul(node_sum, weights[2])


def layer_back(upstream, gain, gathered, pair_pre, node_out, links, weights, halo_rows):
    degree, nodes, width = pair_pre.shape
    normed, inverse = normalize(node_out)
    grad_norm = normalize_back(upstream * gain, normed, inverse).astype(BF16)
    grad_node = right_transposed(grad_norm, weights[2])
    grad_pair_pre = grad_node[None] * silu_slope(pair_pre)
    grad_pair = grad_pair_pre.astype(BF16).reshape(degree * nodes, width)
    grad_self = jnp.sum(grad_pair_pre, axis=0).astype(BF16)
    grad_rows = right_transposed(grad_pair, weights[0]).astype(BF16)
    grad_halo = matmul(hits(links - nodes, halo_rows), grad_rows)
    upstream = upstream + right_transposed(grad_self, weights[1]) + matmul(hits(links, nodes), grad_rows)
    return grad_norm, grad_pair, grad_self, grad_halo.astype(BF16), upstream


def layer_forward(
    latent, halo, links, weights, gains, sends, gathered_out, pair_out, sum_out, node_out, latent_out, sent_out
):
    nodes = latent.shape[0]
    gathered, pair_pre, node_sum, node_pre = layer_values(
        latent[...], halo[...], links[...], weights, pair_out.shape[0]
    )
    normed, _ = normalize(node_pre)
    after = (latent[...].astype(F32) + normed * gains[2:3]).astype(BF16)
    latent_out[...] = after
    sent_out[...] = left_transposed(hits(sends[...], nodes), after).astype(BF16)
    gathered_out[...] = gathered
    pair_out[...] = pair_pre
    sum_out[...] = node_sum
    node_out[...] = node_pre


def layer_last(
    scale,
    latent,
    halo,
    links,
    weights,
    gains,
    cotangent,
    latent_out,
    gathered_out,
    sum_out,
    norm_out,
    pair_out,
    self_out,
    halo_out,
    up_out,
):
    nodes = latent.shape[0]
    gathered, pair_pre, node_sum, node_pre = layer_values(
        latent[...], halo[...], links[...], weights, links.shape[1] // nodes
    )
    normed, _ = normalize(node_pre)
    latent_out[...] = (latent[...].astype(F32) + normed * gains[3:4]).astype(BF16)
    gathered_out[...] = gathered
    sum_out[...] = node_sum
    upstream = cotangent[...].astype(F32) * scale
    norm_out[...], pair_out[...], self_out[...], halo_out[...], up_out[...] = layer_back(
        upstream, gains[3:4], gathered, pair_pre, node_pre, links[...], weights, halo.shape[0]
    )


def layer_first_back(
    upstream,
    returned,
    sends,
    gathered,
    pair_pre,
    node_pre,
    links,
    weights,
    gains,
    norm_out,
    pair_out,
    self_out,
    halo_out,
    up_out,
):
    nodes = upstream.shape[0]
    total = upstream[...] + matmul(hits(sends[...], nodes), returned[...])
    norm_out[...], pair_out[...], self_out[...], halo_out[...], up_out[...] = layer_back(
        total, gains[2:3], gathered[...], pair_pre[...], node_pre[...], links[...], weights, returned.shape[0]
    )


def weight_grads(core, gathered, grad_pair, latent, grad_self, node_sum, grad_norm, kept, sent):
    blocks, _, rows, width = kept.shape
    pairs = ((gathered, grad_pair), (latent, grad_self), (node_sum, grad_norm))
    for place, (rows_in, grads) in enumerate(pairs):
        total = left_transposed(rows_in[...], grads[...]).reshape(blocks, 2, rows, width)
        first = core[0] == 0
        kept[:, place] = jnp.where(first, total[:, 0], total[:, 1]).astype(BF16)
        sent[:, place] = jnp.where(first, total[:, 1], total[:, 0]).astype(BF16)


def add_cores(chip, last_kept, last_other, first_kept, first_other, *outs):
    blocks, rows, _ = last_kept.shape
    pairs = ((last_kept, last_other), (first_kept, first_other))
    for step, out in enumerate(outs):
        place = lax.rem(chip[0] + step, blocks)
        for layer, (kept, other) in enumerate(pairs):
            total = kept[place].astype(F32) + other[place].astype(F32)
            out[pl.ds(layer * rows, rows)] = total.astype(BF16)


def start_back(upstream, returned, sends, mesh_sum, w_node, gains, start_out, sum_out):
    nodes = upstream.shape[0]
    total = upstream[...] + matmul(hits(sends[...], nodes), returned[...])
    normed, inverse = normalize(matmul(mesh_sum[...], w_node[...]))
    grad_start = normalize_back(total * gains[1:2], normed, inverse).astype(BF16)
    start_out[...] = grad_start
    sum_out[...] = right_transposed(grad_start, w_node[...]).astype(BF16)


def edge_back(
    counts,
    core,
    info_west,
    info_own,
    info_east,
    grad_west,
    grad_own,
    grad_east,
    edge_pre,
    edge_rows,
    grid_pre,
    feats,
    sources,
    w_edge,
    gains,
    mesh_sum,
    grad_start,
    kept_out,
    sent_out,
):
    slots = sources.shape[1]
    nodes = grad_own.shape[0]
    channels, grid_nodes = feats.shape
    width = grid_pre.shape[1]
    half = width // 2
    grad_grid = jnp.zeros((grid_nodes, width), F32)
    edge_w = jnp.zeros((width, width), F32)
    sides = ((info_west, grad_west), (info_own, grad_own), (info_east, grad_east))
    for side, (info, grads) in enumerate(sides):
        place = pl.ds(side * slots, slots)
        grad_message = left_transposed(weighted_hits(info[...], nodes), grads[...]).astype(BF16)
        grad_edge = (grad_message.astype(F32) * silu_slope(edge_pre[place])).astype(BF16)
        edge_w += left_transposed(grad_edge, edge_rows[place])
        grad_rows = right_transposed(grad_edge, w_edge[...]).astype(BF16)
        chosen = live_hits(sources[side : side + 1], counts[0, side], grid_nodes)
        grad_grid += matmul(chosen, grad_rows)
    node_w = left_transposed(grad_start[...], mesh_sum[...])
    values = grid_pre[...]
    normed, inverse = normalize(silu(values))
    grad_act = (normalize_back(grad_grid * gains[0:1], normed, inverse) * silu_slope(values)).astype(BF16)
    embed = matmul(feats[...], grad_act)
    spare = 2 * EMBED_HALF - channels
    embed = jnp.concatenate([embed, jnp.zeros((spare, width), F32)], axis=0).T
    low = jnp.concatenate([edge_w[:, :half], node_w[:, :half], embed[:, :EMBED_HALF]], axis=1).astype(BF16)
    high = jnp.concatenate([edge_w[:, half:], node_w[:, half:], embed[:, EMBED_HALF:]], axis=1).astype(BF16)

    @pl.when(core[0] == 0)
    def _():
        kept_out[...] = low
        sent_out[...] = high

    @pl.when(core[0] != 0)
    def _():
        kept_out[...] = high
        sent_out[...] = low


EMBED_HALF = 128


def pack(kept, other, *refs):
    blocks, out = refs[:-1], refs[-1]
    rows = blocks[0].shape[0]
    total = sum(block[...].astype(F32) for block in blocks)
    out[:, :rows] = total.T.astype(BF16)
    out[:, rows:] = (kept[...].astype(F32) + other[...].astype(F32)).astype(BF16)


def sum_blocks(blocks, out):
    total = jnp.sum(blocks[...].astype(F32), axis=0).astype(BF16)
    out[...] = jnp.broadcast_to(total[None], out.shape)


def local(
    grid_feats,
    g2m_src,
    g2m_count,
    g2m_dst,
    g2m_weight,
    halo_send,
    mesh_src,
    cotangent,
    w_embed,
    w_encode,
    w_layers,
    gains,
):
    peers = lax.axis_size("mesh")
    bands = lax.axis_size("grid")
    nodes, degree = mesh_src.shape
    grid_nodes, channels = grid_feats.shape
    width = w_embed.shape[1]
    slots = g2m_src.shape[1]
    halo_rows = halo_send.size
    columns = width // peers
    pairs = nodes * degree
    layers = w_layers.shape[0]
    unit = 2 * width * width
    band = lax.axis_index("grid").astype(jnp.int32)
    core = (band % 2).reshape(1)
    chip = (band // 2).reshape(1)
    sends = halo_send.reshape(1, -1)
    links = mesh_src.T.reshape(1, -1)
    feats = grid_feats.T

    edge_info = jnp.stack([g2m_dst.astype(F32), g2m_weight.astype(F32)], axis=1)
    info_west, info_east = from_sides(edge_info[2], edge_info[0])
    info = [info_west, edge_info[1], info_east]
    grid_pre, edge_rows, edge_pre, messages = call(
        edge_forward,
        [
            ((grid_nodes, width), F32),
            ((3 * slots, width), BF16),
            ((3 * slots, width), F32),
            ((3 * slots, width), BF16),
        ],
        [g2m_count, feats, g2m_src, w_embed, w_encode, gains],
        unit * 8 * slots,
        scalars=(0,),
        picked={4: 0},
    )
    sum_west, sum_own, sum_east = call(
        edge_sums,
        [((nodes, width), BF16), ((nodes, width), F32), ((nodes, width), BF16)],
        [*info, messages],
        unit * slots,
    )
    got_west, got_east = from_sides(sum_east, sum_west)
    mesh_sum, latent, sent = call(
        mesh_start,
        [((nodes, width), BF16), ((nodes, width), BF16), ((halo_rows, width), BF16)],
        [sum_own, got_west, got_east, w_encode, gains, sends],
        unit * nodes * 2,
        picked={3: 1},
    )
    halo = exchange(sent.reshape(peers, -1, width), "mesh").reshape(-1, width)
    gathered, pair_pre, node_sum, node_pre, middle, sent = call(
        layer_forward,
        [
            ((pairs, width), BF16),
            ((degree, nodes, width), F32),
            ((nodes, width), BF16),
            ((nodes, width), F32),
            ((nodes, width), BF16),
            ((halo_rows, width), BF16),
        ],
        [latent, halo, links, w_layers, gains, sends],
        unit * pairs * 2,
        picked={3: 0},
    )
    halo = exchange(sent.reshape(peers, -1, width), "mesh").reshape(-1, width)
    loss_scale = jnp.full((1,), 1.0 / math.sqrt(nodes * bands * peers), F32)
    back_shapes = [
        ((nodes, width), BF16),
        ((pairs, width), BF16),
        ((nodes, width), BF16),
        ((halo_rows, width), BF16),
        ((nodes, width), F32),
    ]

    def core_halves(*arrays):
        shape = (bands // 2, 3, width // bands, width)
        kept, sent = call(
            weight_grads, [(shape, BF16)] * 2, [core, *arrays], unit * (pairs + 2 * nodes), scalars=(0,)
        )
        rows = (bands // 2, 3 * width // bands, width)
        return kept.reshape(rows), to_other_core(sent).reshape(rows)

    def last_layer(scale, *refs):
        layer_last(scale[0], *refs)

    mesh_out, last_gathered, last_sum, last_norm, last_pair, last_self, grad_halo, upstream = call(
        last_layer,
        [((nodes, width), BF16), ((pairs, width), BF16), ((nodes, width), BF16)] + back_shapes,
        [loss_scale, middle, halo, links, w_layers, gains, cotangent],
        unit * pairs * 4,
        scalars=(0,),
        picked={4: 1},
    )
    returned = exchange(grad_halo.reshape(peers, -1, width), "mesh").reshape(-1, width)
    last_rows = core_halves(last_gathered, last_pair, middle, last_self, last_sum, last_norm)
    returned, last_rows = lax.optimization_barrier((returned, last_rows))
    grad_norm, grad_pair, grad_self, grad_halo, upstream = call(
        layer_first_back,
        back_shapes,
        [upstream, returned, sends, gathered, pair_pre, node_pre, links, w_layers, gains],
        unit * pairs * 3,
        picked={7: 0},
    )
    returned = exchange(grad_halo.reshape(peers, -1, width), "mesh").reshape(-1, width)
    first_rows = core_halves(gathered, grad_pair, latent, grad_self, node_sum, grad_norm)
    chips = bands // 2
    shared = 6 * width // bands
    parts = call(
        add_cores, [((shared, width), BF16)] * chips, [chip, *last_rows, *first_rows], 0, scalars=(0,)
    )
    returned, parts = lax.optimization_barrier((returned, parts))
    grad_start, grad_sum = call(
        start_back,
        [((nodes, width), BF16), ((nodes, width), BF16)],
        [upstream, returned, sends, mesh_sum, w_encode, gains],
        unit * nodes * 3,
        picked={4: 1},
    )
    grad_west, grad_east = from_sides(grad_sum, grad_sum)
    grad_sum, parts = lax.optimization_barrier((grad_sum, parts))
    parts = [parts[0]] + [along_y(parts[step], step) for step in range(1, chips)]
    part = width + EMBED_HALF
    kept, passed = call(
        edge_back,
        [((width, part), BF16), ((width, part), BF16)],
        [
            g2m_count,
            core,
            *info,
            grad_west,
            grad_sum,
            grad_east,
            edge_pre,
            edge_rows,
            grid_pre,
            feats,
            g2m_src,
            w_encode,
            gains,
            mesh_sum,
            grad_start,
        ],
        unit * 12 * slots,
        scalars=(0, 1),
        picked={13: 0},
    )
    kept, passed, parts = lax.optimization_barrier((kept, passed, parts))
    other = to_other_core(passed)
    (packed,) = call(
        pack, [((width, shared + part), BF16)], [kept, other, *parts], 0
    )
    arrived = exchange(packed.reshape(peers, columns, -1), "mesh")
    (summed,) = call(sum_blocks, [((bands, columns, shared + part), BF16)], [arrived], 0)
    held = exchange(summed, "grid")
    tail = held[:, :, shared:].reshape(bands // 2, 2, columns, part).astype(F32)
    tail = jnp.sum(tail, axis=0)
    half = width // 2
    embed = jnp.concatenate([tail[0, :, width:], tail[1, :, width:]], axis=1)
    embed = spread(embed.astype(BF16), "mesh")
    total_embed = embed.reshape(width, -1).T[:channels].astype(F32)
    edge_w = jnp.concatenate([tail[0, :, :half], tail[1, :, :half]], axis=1).T
    node_w = jnp.concatenate([tail[0, :, half:width], tail[1, :, half:width]], axis=1).T
    whole = held[:, :, :shared].reshape(bands, columns, layers, 3, width // bands)
    whole = whole[:, :, ::-1].transpose(2, 3, 1, 0, 4).reshape(layers, 3, columns, width).swapaxes(2, 3)
    return mesh_out, whole.astype(F32), jnp.stack([edge_w, node_w]), total_embed


def solution(mesh):
    placed = (P(("grid", "mesh"), None),) * 8 + (P(),) * 4
    return jax.shard_map(
        local,
        mesh=mesh,
        in_specs=placed,
        out_specs=(
            P(("grid", "mesh"), None),
            P(None, None, None, "mesh"),
            P(None, None, "mesh"),
            P(),
        ),
        check_vma=False,
    )
```

```python
import math

import jax
import jax.numpy as jnp
from jax import lax
from jax.experimental import pallas as pl
from jax.experimental.pallas import tpu as pltpu
from jax.sharding import PartitionSpec as P

NORM_EPSILON = 1e-05
BF16 = jnp.bfloat16
F32 = jnp.float32


def side_pairs(count):
    forward = [(i, (i + 1) % count) for i in range(count)]
    backward = [((i + 1) % count, i) for i in range(count)]
    return forward, backward


def from_sides(to_east, to_west):
    forward, backward = side_pairs(lax.axis_size("mesh"))
    return lax.ppermute(to_east, "mesh", forward), lax.ppermute(to_west, "mesh", backward)


def exchange(blocks, axis):
    return lax.all_to_all(blocks, axis, split_axis=0, concat_axis=0, tiled=True)


def spread(block, axis):
    count = lax.axis_size(axis)
    return exchange(jnp.broadcast_to(block[None], (count,) + block.shape), axis)


def along_y(block, step):
    count = lax.axis_size("grid")
    return lax.ppermute(block, "grid", [(i, (i + 2 * step) % count) for i in range(count)])


def to_other_core(block):
    return lax.ppermute(block, "grid", [(i, i ^ 1) for i in range(lax.axis_size("grid"))])


def normalize(values):
    average = jnp.mean(values, axis=-1, keepdims=True)
    centred = values - average
    inverse = lax.rsqrt(jnp.mean(centred * centred, axis=-1, keepdims=True) + NORM_EPSILON)
    return (centred * inverse, inverse)


def normalize_back(grad_hat, normed, inverse):
    first = jnp.mean(grad_hat, axis=-1, keepdims=True)
    second = jnp.mean(grad_hat * normed, axis=-1, keepdims=True)
    return inverse * (grad_hat - first - normed * second)


def silu(values):
    return values * jax.nn.sigmoid(values)


def silu_slope(values):
    return silu_both(values)[1]


def silu_both(values):
    logistic = jax.nn.sigmoid(values)
    return values * logistic, logistic * (1.0 + values * (1.0 - logistic))


def matmul(matrix_a, matrix_b):
    return jnp.dot(matrix_a, matrix_b, preferred_element_type=F32)


def left_transposed(matrix_a, matrix_b):
    return lax.dot_general(
        matrix_a, matrix_b, (((0,), (0,)), ((), ())), preferred_element_type=F32
    )


def right_transposed(matrix_a, matrix_b):
    return lax.dot_general(
        matrix_a, matrix_b, (((1,), (1,)), ((), ())), preferred_element_type=F32
    )


def hits(index_row, count):
    rows = lax.broadcasted_iota(jnp.int32, (count, index_row.shape[1]), 0)
    return jnp.where(rows == index_row, 1.0, 0.0).astype(BF16)


def weighted_hits(info, count):
    rows = lax.broadcasted_iota(jnp.int32, (count, info.shape[1]), 0).astype(F32)
    return jnp.where(rows == info[0:1], info[1:2], 0.0).astype(BF16)


def live_hits(index_row, live, count):
    shape = (count, index_row.shape[1])
    rows = lax.broadcasted_iota(jnp.int32, shape, 0)
    slots = lax.broadcasted_iota(jnp.int32, shape, 1)
    return jnp.where((rows == index_row) & (slots < live), 1.0, 0.0).astype(BF16)


def call(kernel, outs, args, flops, scalars=(), picked=None):
    picked = picked or {}
    specs = []
    for place, arg in enumerate(args):
        if place in scalars:
            specs.append(pl.BlockSpec(memory_space=pltpu.SMEM))
        elif place in picked:
            lead, zeros = picked[place], (0,) * (arg.ndim - 1)
            specs.append(
                pl.BlockSpec((None,) + arg.shape[1:], lambda i, lead=lead, zeros=zeros: (lead,) + zeros)
            )
        else:
            specs.append(pl.BlockSpec(arg.shape, lambda i, zeros=(0,) * arg.ndim: zeros))
    shapes = [jax.ShapeDtypeStruct(shape, dtype) for shape, dtype in outs]
    moved = sum(math.prod(s.shape) * s.dtype.itemsize for s in list(args) + shapes)
    return pl.pallas_call(
        kernel,
        grid=(1,),
        in_specs=specs,
        out_specs=[
            pl.BlockSpec(s.shape, lambda i, zeros=(0,) * len(s.shape): zeros) for s in shapes
        ],
        out_shape=shapes,
        compiler_params=pltpu.CompilerParams(vmem_limit_bytes=64 * 2**20),
        cost_estimate=pl.CostEstimate(flops=flops, bytes_accessed=moved, transcendentals=0),
    )(*args)


def edge_forward(counts, feats, sources, w_embed, w_edge, gains, pre_out, rows_out, slope_out, message_out):
    grid_pre = left_transposed(feats[...], w_embed[...])
    pre_out[...] = grid_pre
    normed, _ = normalize(silu(grid_pre))
    latent = (normed * gains[0:1]).astype(BF16)
    slots = sources.shape[1]
    for side in range(3):
        chosen = live_hits(sources[side : side + 1], counts[0, side], latent.shape[0])
        rows = left_transposed(chosen, latent).astype(BF16)
        message, slope = silu_both(matmul(rows, w_edge[...]))
        place = pl.ds(side * slots, slots)
        rows_out[place] = rows
        slope_out[place] = slope.astype(BF16)
        message_out[place] = message.astype(BF16)


def edge_sums(info_west, info_own, info_east, messages, west_out, own_out, east_out):
    nodes = own_out.shape[0]
    slots = info_own.shape[1]
    sides = ((info_west, west_out), (info_own, own_out), (info_east, east_out))
    for side, (info, out) in enumerate(sides):
        total = matmul(weighted_hits(info[...], nodes), messages[pl.ds(side * slots, slots)])
        out[...] = total.astype(out.dtype)


def mesh_start(own, west, east, w_node, gains, sends, sum_out, latent_out, sent_out):
    mesh_sum = (own[...] + west[...].astype(F32) + east[...].astype(F32)).astype(BF16)
    sum_out[...] = mesh_sum
    normed, _ = normalize(matmul(mesh_sum, w_node[...]))
    latent = (normed * gains[1:2]).astype(BF16)
    latent_out[...] = latent
    sent_out[...] = left_transposed(hits(sends[...], latent.shape[0]), latent).astype(BF16)


def layer_values(latent, halo, links, weights, degree):
    nodes, width = latent.shape
    own = left_transposed(hits(links, nodes), latent)
    far = left_transposed(hits(links - nodes, halo.shape[0]), halo)
    gathered = (own + far).astype(BF16)
    pair_pre = matmul(gathered, weights[0]).reshape(degree, nodes, width) + matmul(latent, weights[1])[None]
    message, slope = silu_both(pair_pre)
    node_sum = jnp.sum(message.astype(BF16).astype(F32), axis=0).astype(BF16)
    return gathered, slope, node_sum, matmul(node_sum, weights[2])


def layer_back(upstream, gain, gathered, slope, node_out, links, weights, halo_rows):
    degree, nodes, width = slope.shape
    normed, inverse = normalize(node_out)
    grad_norm = normalize_back(upstream * gain, normed, inverse).astype(BF16)
    grad_node = right_transposed(grad_norm, weights[2])
    grad_pair_pre = grad_node[None] * slope
    grad_pair = grad_pair_pre.astype(BF16).reshape(degree * nodes, width)
    grad_self = jnp.sum(grad_pair_pre, axis=0).astype(BF16)
    grad_rows = right_transposed(grad_pair, weights[0]).astype(BF16)
    grad_halo = matmul(hits(links - nodes, halo_rows), grad_rows)
    upstream = upstream + right_transposed(grad_self, weights[1]) + matmul(hits(links, nodes), grad_rows)
    return grad_norm, grad_pair, grad_self, grad_halo.astype(BF16), upstream


def layer_forward(
    latent, halo, links, weights, gains, sends, gathered_out, slope_out, sum_out, node_out, latent_out, sent_out
):
    nodes = latent.shape[0]
    gathered, slope, node_sum, node_pre = layer_values(
        latent[...], halo[...], links[...], weights, slope_out.shape[0]
    )
    normed, _ = normalize(node_pre)
    after = (latent[...].astype(F32) + normed * gains[2:3]).astype(BF16)
    latent_out[...] = after
    sent_out[...] = left_transposed(hits(sends[...], nodes), after).astype(BF16)
    gathered_out[...] = gathered
    slope_out[...] = slope.astype(BF16)
    sum_out[...] = node_sum
    node_out[...] = node_pre


def layer_last(
    scale,
    latent,
    halo,
    links,
    weights,
    gains,
    cotangent,
    latent_out,
    gathered_out,
    sum_out,
    norm_out,
    pair_out,
    self_out,
    halo_out,
    up_out,
):
    nodes = latent.shape[0]
    gathered, slope, node_sum, node_pre = layer_values(
        latent[...], halo[...], links[...], weights, links.shape[1] // nodes
    )
    normed, _ = normalize(node_pre)
    latent_out[...] = (latent[...].astype(F32) + normed * gains[3:4]).astype(BF16)
    gathered_out[...] = gathered
    sum_out[...] = node_sum
    upstream = cotangent[...].astype(F32) * scale
    norm_out[...], pair_out[...], self_out[...], halo_out[...], up_out[...] = layer_back(
        upstream, gains[3:4], gathered, slope, node_pre, links[...], weights, halo.shape[0]
    )


def layer_first_back(
    upstream,
    returned,
    sends,
    gathered,
    slope,
    node_pre,
    links,
    weights,
    gains,
    norm_out,
    pair_out,
    self_out,
    halo_out,
    up_out,
):
    nodes = upstream.shape[0]
    total = upstream[...] + matmul(hits(sends[...], nodes), returned[...])
    norm_out[...], pair_out[...], self_out[...], halo_out[...], up_out[...] = layer_back(
        total, gains[2:3], gathered[...], slope[...].astype(F32), node_pre[...], links[...], weights, returned.shape[0]
    )


def weight_grads(core, gathered, grad_pair, latent, grad_self, node_sum, grad_norm, kept, sent):
    blocks, _, rows, width = kept.shape
    pairs = ((gathered, grad_pair), (latent, grad_self), (node_sum, grad_norm))
    for place, (rows_in, grads) in enumerate(pairs):
        total = left_transposed(rows_in[...], grads[...]).reshape(blocks, 2, rows, width)
        first = core[0] == 0
        kept[:, place] = jnp.where(first, total[:, 0], total[:, 1]).astype(BF16)
        sent[:, place] = jnp.where(first, total[:, 1], total[:, 0]).astype(BF16)


def add_cores(chip, last_kept, last_other, first_kept, first_other, *outs):
    blocks, rows, _ = last_kept.shape
    pairs = ((last_kept, last_other), (first_kept, first_other))
    for step, out in enumerate(outs):
        place = lax.rem(chip[0] + step, blocks)
        for layer, (kept, other) in enumerate(pairs):
            total = kept[place].astype(F32) + other[place].astype(F32)
            out[pl.ds(layer * rows, rows)] = total.astype(BF16)


def start_back(upstream, returned, sends, mesh_sum, w_node, gains, start_out, sum_out):
    nodes = upstream.shape[0]
    total = upstream[...] + matmul(hits(sends[...], nodes), returned[...])
    normed, inverse = normalize(matmul(mesh_sum[...], w_node[...]))
    grad_start = normalize_back(total * gains[1:2], normed, inverse).astype(BF16)
    start_out[...] = grad_start
    sum_out[...] = right_transposed(grad_start, w_node[...]).astype(BF16)


def edge_back(
    counts,
    core,
    info_west,
    info_own,
    info_east,
    grad_west,
    grad_own,
    grad_east,
    edge_slope,
    edge_rows,
    grid_pre,
    feats,
    sources,
    w_edge,
    gains,
    mesh_sum,
    grad_start,
    kept_out,
    sent_out,
):
    slots = sources.shape[1]
    nodes = grad_own.shape[0]
    channels, grid_nodes = feats.shape
    width = grid_pre.shape[1]
    half = width // 2
    grad_grid = jnp.zeros((grid_nodes, width), F32)
    edge_w = jnp.zeros((width, width), F32)
    sides = ((info_west, grad_west), (info_own, grad_own), (info_east, grad_east))
    for side, (info, grads) in enumerate(sides):
        place = pl.ds(side * slots, slots)
        grad_message = left_transposed(weighted_hits(info[...], nodes), grads[...]).astype(BF16)
        grad_edge = (grad_message.astype(F32) * edge_slope[place].astype(F32)).astype(BF16)
        edge_w += left_transposed(grad_edge, edge_rows[place])
        grad_rows = right_transposed(grad_edge, w_edge[...]).astype(BF16)
        chosen = live_hits(sources[side : side + 1], counts[0, side], grid_nodes)
        grad_grid += matmul(chosen, grad_rows)
    node_w = left_transposed(grad_start[...], mesh_sum[...])
    values = grid_pre[...]
    normed, inverse = normalize(silu(values))
    grad_act = (normalize_back(grad_grid * gains[0:1], normed, inverse) * silu_slope(values)).astype(BF16)
    embed = matmul(feats[...], grad_act)
    spare = 2 * EMBED_HALF - channels
    embed = jnp.concatenate([embed, jnp.zeros((spare, width), F32)], axis=0).T
    low = jnp.concatenate([edge_w[:, :half], node_w[:, :half], embed[:, :EMBED_HALF]], axis=1).astype(BF16)
    high = jnp.concatenate([edge_w[:, half:], node_w[:, half:], embed[:, EMBED_HALF:]], axis=1).astype(BF16)

    @pl.when(core[0] == 0)
    def _():
        kept_out[...] = low
        sent_out[...] = high

    @pl.when(core[0] != 0)
    def _():
        kept_out[...] = high
        sent_out[...] = low


EMBED_HALF = 128


def pack(kept, other, *refs):
    blocks, out = refs[:-1], refs[-1]
    rows = blocks[0].shape[0]
    total = sum(block[...].astype(F32) for block in blocks)
    out[:, :rows] = total.T.astype(BF16)
    out[:, rows:] = (kept[...].astype(F32) + other[...].astype(F32)).astype(BF16)


def sum_blocks(blocks, out):
    total = jnp.sum(blocks[...].astype(F32), axis=0).astype(BF16)
    out[...] = jnp.broadcast_to(total[None], out.shape)


def local(
    grid_feats,
    g2m_src,
    g2m_count,
    g2m_dst,
    g2m_weight,
    halo_send,
    mesh_src,
    cotangent,
    w_embed,
    w_encode,
    w_layers,
    gains,
):
    peers = lax.axis_size("mesh")
    bands = lax.axis_size("grid")
    nodes, degree = mesh_src.shape
    grid_nodes, channels = grid_feats.shape
    width = w_embed.shape[1]
    slots = g2m_src.shape[1]
    halo_rows = halo_send.size
    columns = width // peers
    pairs = nodes * degree
    layers = w_layers.shape[0]
    unit = 2 * width * width
    band = lax.axis_index("grid").astype(jnp.int32)
    core = (band % 2).reshape(1)
    chip = (band // 2).reshape(1)
    sends = halo_send.reshape(1, -1)
    links = mesh_src.T.reshape(1, -1)
    feats = grid_feats.T

    edge_info = jnp.stack([g2m_dst.astype(F32), g2m_weight.astype(F32)], axis=1)
    info_west, info_east = from_sides(edge_info[2], edge_info[0])
    info = [info_west, edge_info[1], info_east]
    grid_pre, edge_rows, edge_slope, messages = call(
        edge_forward,
        [
            ((grid_nodes, width), F32),
            ((3 * slots, width), BF16),
            ((3 * slots, width), BF16),
            ((3 * slots, width), BF16),
        ],
        [g2m_count, feats, g2m_src, w_embed, w_encode, gains],
        unit * 8 * slots,
        scalars=(0,),
        picked={4: 0},
    )
    sum_west, sum_own, sum_east = call(
        edge_sums,
        [((nodes, width), BF16), ((nodes, width), F32), ((nodes, width), BF16)],
        [*info, messages],
        unit * slots,
    )
    got_west, got_east = from_sides(sum_east, sum_west)
    mesh_sum, latent, sent = call(
        mesh_start,
        [((nodes, width), BF16), ((nodes, width), BF16), ((halo_rows, width), BF16)],
        [sum_own, got_west, got_east, w_encode, gains, sends],
        unit * nodes * 2,
        picked={3: 1},
    )
    halo = exchange(sent.reshape(peers, -1, width), "mesh").reshape(-1, width)
    gathered, pair_slope, node_sum, node_pre, middle, sent = call(
        layer_forward,
        [
            ((pairs, width), BF16),
            ((degree, nodes, width), BF16),
            ((nodes, width), BF16),
            ((nodes, width), F32),
            ((nodes, width), BF16),
            ((halo_rows, width), BF16),
        ],
        [latent, halo, links, w_layers, gains, sends],
        unit * pairs * 2,
        picked={3: 0},
    )
    halo = exchange(sent.reshape(peers, -1, width), "mesh").reshape(-1, width)
    loss_scale = jnp.full((1,), 1.0 / math.sqrt(nodes * bands * peers), F32)
    back_shapes = [
        ((nodes, width), BF16),
        ((pairs, width), BF16),
        ((nodes, width), BF16),
        ((halo_rows, width), BF16),
        ((nodes, width), F32),
    ]

    def core_halves(*arrays):
        shape = (bands // 2, 3, width // bands, width)
        kept, sent = call(
            weight_grads, [(shape, BF16)] * 2, [core, *arrays], unit * (pairs + 2 * nodes), scalars=(0,)
        )
        rows = (bands // 2, 3 * width // bands, width)
        return kept.reshape(rows), to_other_core(sent).reshape(rows)

    def last_layer(scale, *refs):
        layer_last(scale[0], *refs)

    mesh_out, last_gathered, last_sum, last_norm, last_pair, last_self, grad_halo, upstream = call(
        last_layer,
        [((nodes, width), BF16), ((pairs, width), BF16), ((nodes, width), BF16)] + back_shapes,
        [loss_scale, middle, halo, links, w_layers, gains, cotangent],
        unit * pairs * 4,
        scalars=(0,),
        picked={4: 1},
    )
    returned = exchange(grad_halo.reshape(peers, -1, width), "mesh").reshape(-1, width)
    last_rows = core_halves(last_gathered, last_pair, middle, last_self, last_sum, last_norm)
    returned, last_rows = lax.optimization_barrier((returned, last_rows))
    grad_norm, grad_pair, grad_self, grad_halo, upstream = call(
        layer_first_back,
        back_shapes,
        [upstream, returned, sends, gathered, pair_slope, node_pre, links, w_layers, gains],
        unit * pairs * 3,
        picked={7: 0},
    )
    returned = exchange(grad_halo.reshape(peers, -1, width), "mesh").reshape(-1, width)
    first_rows = core_halves(gathered, grad_pair, latent, grad_self, node_sum, grad_norm)
    chips = bands // 2
    shared = 6 * width // bands
    parts = call(
        add_cores, [((shared, width), BF16)] * chips, [chip, *last_rows, *first_rows], 0, scalars=(0,)
    )
    returned, parts = lax.optimization_barrier((returned, parts))
    grad_start, grad_sum = call(
        start_back,
        [((nodes, width), BF16), ((nodes, width), BF16)],
        [upstream, returned, sends, mesh_sum, w_encode, gains],
        unit * nodes * 3,
        picked={4: 1},
    )
    grad_west, grad_east = from_sides(grad_sum, grad_sum)
    grad_sum, parts = lax.optimization_barrier((grad_sum, parts))
    parts = [parts[0]] + [along_y(parts[step], step) for step in range(1, chips)]
    part = width + EMBED_HALF
    kept, passed = call(
        edge_back,
        [((width, part), BF16), ((width, part), BF16)],
        [
            g2m_count,
            core,
            *info,
            grad_west,
            grad_sum,
            grad_east,
            edge_slope,
            edge_rows,
            grid_pre,
            feats,
            g2m_src,
            w_encode,
            gains,
            mesh_sum,
            grad_start,
        ],
        unit * 12 * slots,
        scalars=(0, 1),
        picked={13: 0},
    )
    kept, passed, parts = lax.optimization_barrier((kept, passed, parts))
    other = to_other_core(passed)
    (packed,) = call(
        pack, [((width, shared + part), BF16)], [kept, other, *parts], 0
    )
    arrived = exchange(packed.reshape(peers, columns, -1), "mesh")
    (summed,) = call(sum_blocks, [((bands, columns, shared + part), BF16)], [arrived], 0)
    held = exchange(summed, "grid")
    tail = held[:, :, shared:].reshape(bands // 2, 2, columns, part).astype(F32)
    tail = jnp.sum(tail, axis=0)
    half = width // 2
    embed = jnp.concatenate([tail[0, :, width:], tail[1, :, width:]], axis=1)
    embed = spread(embed.astype(BF16), "mesh")
    total_embed = embed.reshape(width, -1).T[:channels].astype(F32)
    edge_w = jnp.concatenate([tail[0, :, :half], tail[1, :, :half]], axis=1).T
    node_w = jnp.concatenate([tail[0, :, half:width], tail[1, :, half:width]], axis=1).T
    whole = held[:, :, :shared].reshape(bands, columns, layers, 3, width // bands)
    whole = whole[:, :, ::-1].transpose(2, 3, 1, 0, 4).reshape(layers, 3, columns, width).swapaxes(2, 3)
    return mesh_out, whole.astype(F32), jnp.stack([edge_w, node_w]), total_embed


def solution(mesh):
    placed = (P(("grid", "mesh"), None),) * 8 + (P(),) * 4
    return jax.shard_map(
        local,
        mesh=mesh,
        in_specs=placed,
        out_specs=(
            P(("grid", "mesh"), None),
            P(None, None, None, "mesh"),
            P(None, None, "mesh"),
            P(),
        ),
        check_vma=False,
    )
```

```python
import math

import jax
import jax.numpy as jnp
from jax import lax
from jax.experimental import pallas as pl
from jax.experimental.pallas import tpu as pltpu
from jax.sharding import PartitionSpec as P

NORM_EPSILON = 1e-05
BF16 = jnp.bfloat16
F32 = jnp.float32


def side_pairs(count):
    forward = [(i, (i + 1) % count) for i in range(count)]
    backward = [((i + 1) % count, i) for i in range(count)]
    return forward, backward


def from_sides(to_east, to_west):
    forward, backward = side_pairs(lax.axis_size("mesh"))
    return lax.ppermute(to_east, "mesh", forward), lax.ppermute(to_west, "mesh", backward)


def exchange(blocks, axis):
    return lax.all_to_all(blocks, axis, split_axis=0, concat_axis=0, tiled=True)


def spread(block, axis):
    count = lax.axis_size(axis)
    return exchange(jnp.broadcast_to(block[None], (count,) + block.shape), axis)


def along_y(block, step):
    count = lax.axis_size("grid")
    return lax.ppermute(block, "grid", [(i, (i + 2 * step) % count) for i in range(count)])


def to_other_core(block):
    return lax.ppermute(block, "grid", [(i, i ^ 1) for i in range(lax.axis_size("grid"))])


def normalize(values):
    average = jnp.mean(values, axis=-1, keepdims=True)
    centred = values - average
    inverse = lax.rsqrt(jnp.mean(centred * centred, axis=-1, keepdims=True) + NORM_EPSILON)
    return (centred * inverse, inverse)


def normalize_back(grad_hat, normed, inverse):
    first = jnp.mean(grad_hat, axis=-1, keepdims=True)
    second = jnp.mean(grad_hat * normed, axis=-1, keepdims=True)
    return inverse * (grad_hat - first - normed * second)


def silu(values):
    return values * jax.nn.sigmoid(values)


def silu_slope(values):
    return silu_both(values)[1]


def silu_both(values):
    logistic = jax.nn.sigmoid(values)
    return values * logistic, logistic * (1.0 + values * (1.0 - logistic))


def matmul(matrix_a, matrix_b):
    return jnp.dot(matrix_a, matrix_b, preferred_element_type=F32)


def left_transposed(matrix_a, matrix_b):
    return lax.dot_general(
        matrix_a, matrix_b, (((0,), (0,)), ((), ())), preferred_element_type=F32
    )


def right_transposed(matrix_a, matrix_b):
    return lax.dot_general(
        matrix_a, matrix_b, (((1,), (1,)), ((), ())), preferred_element_type=F32
    )


def hits(index_row, count):
    rows = lax.broadcasted_iota(jnp.int32, (count, index_row.shape[1]), 0)
    return jnp.where(rows == index_row, 1.0, 0.0).astype(BF16)


def weighted_hits(info, count):
    rows = lax.broadcasted_iota(jnp.int32, (count, info.shape[1]), 0).astype(F32)
    return jnp.where(rows == info[0:1], info[1:2], 0.0).astype(BF16)


def live_hits(index_row, live, count):
    shape = (count, index_row.shape[1])
    rows = lax.broadcasted_iota(jnp.int32, shape, 0)
    slots = lax.broadcasted_iota(jnp.int32, shape, 1)
    return jnp.where((rows == index_row) & (slots < live), 1.0, 0.0).astype(BF16)


def call(kernel, outs, args, flops, scalars=(), picked=None):
    picked = picked or {}
    specs = []
    for place, arg in enumerate(args):
        if place in scalars:
            specs.append(pl.BlockSpec(memory_space=pltpu.SMEM))
        elif place in picked:
            lead, zeros = picked[place], (0,) * (arg.ndim - 1)
            specs.append(
                pl.BlockSpec((None,) + arg.shape[1:], lambda i, lead=lead, zeros=zeros: (lead,) + zeros)
            )
        else:
            specs.append(pl.BlockSpec(arg.shape, lambda i, zeros=(0,) * arg.ndim: zeros))
    shapes = [jax.ShapeDtypeStruct(shape, dtype) for shape, dtype in outs]
    moved = sum(math.prod(s.shape) * s.dtype.itemsize for s in list(args) + shapes)
    return pl.pallas_call(
        kernel,
        grid=(1,),
        in_specs=specs,
        out_specs=[
            pl.BlockSpec(s.shape, lambda i, zeros=(0,) * len(s.shape): zeros) for s in shapes
        ],
        out_shape=shapes,
        compiler_params=pltpu.CompilerParams(vmem_limit_bytes=64 * 2**20),
        cost_estimate=pl.CostEstimate(flops=flops, bytes_accessed=moved, transcendentals=0),
    )(*args)


def edge_forward(counts, feats, sources, w_embed, w_edge, gains, pre_out, rows_out, slope_out, message_out):
    grid_pre = left_transposed(feats[...], w_embed[...])
    pre_out[...] = grid_pre
    normed, _ = normalize(silu(grid_pre))
    latent = (normed * gains[0:1]).astype(BF16)
    slots = sources.shape[1]
    for side in range(3):
        chosen = live_hits(sources[side : side + 1], counts[0, side], latent.shape[0])
        rows = left_transposed(chosen, latent).astype(BF16)
        message, slope = silu_both(matmul(rows, w_edge[...]))
        place = pl.ds(side * slots, slots)
        rows_out[place] = rows
        slope_out[place] = slope.astype(BF16)
        message_out[place] = message.astype(BF16)


def edge_sums(info_west, info_own, info_east, messages, west_out, own_out, east_out):
    nodes = own_out.shape[0]
    slots = info_own.shape[1]
    sides = ((info_west, west_out), (info_own, own_out), (info_east, east_out))
    for side, (info, out) in enumerate(sides):
        total = matmul(weighted_hits(info[...], nodes), messages[pl.ds(side * slots, slots)])
        out[...] = total.astype(out.dtype)


def mesh_start(own, west, east, w_node, gains, sends, sum_out, latent_out, sent_out):
    mesh_sum = (own[...] + west[...].astype(F32) + east[...].astype(F32)).astype(BF16)
    sum_out[...] = mesh_sum
    normed, _ = normalize(matmul(mesh_sum, w_node[...]))
    latent = (normed * gains[1:2]).astype(BF16)
    latent_out[...] = latent
    sent_out[...] = left_transposed(hits(sends[...], latent.shape[0]), latent).astype(BF16)


def layer_values(latent, halo, links, weights, degree):
    nodes, width = latent.shape
    own = left_transposed(hits(links, nodes), latent)
    far = left_transposed(hits(links - nodes, halo.shape[0]), halo)
    gathered = (own + far).astype(BF16)
    pair_pre = matmul(gathered, weights[0]).reshape(degree, nodes, width) + matmul(latent, weights[1])[None]
    message, slope = silu_both(pair_pre)
    node_sum = jnp.sum(message.astype(BF16).astype(F32), axis=0).astype(BF16)
    return gathered, slope, node_sum, matmul(node_sum, weights[2])


def layer_back(upstream, gain, gathered, slope, node_out, links, weights, halo_rows):
    degree, nodes, width = slope.shape
    normed, inverse = normalize(node_out)
    grad_norm = normalize_back(upstream * gain, normed, inverse).astype(BF16)
    grad_node = right_transposed(grad_norm, weights[2])
    grad_pair_pre = grad_node[None] * slope
    grad_pair = grad_pair_pre.astype(BF16).reshape(degree * nodes, width)
    grad_self = jnp.sum(grad_pair_pre, axis=0).astype(BF16)
    grad_rows = right_transposed(grad_pair, weights[0]).astype(BF16)
    grad_halo = matmul(hits(links - nodes, halo_rows), grad_rows)
    upstream = upstream + right_transposed(grad_self, weights[1]) + matmul(hits(links, nodes), grad_rows)
    return grad_norm, grad_pair, grad_self, grad_halo.astype(BF16), upstream


def layer_forward(
    latent, halo, links, weights, gains, sends, gathered_out, slope_out, sum_out, node_out, latent_out, sent_out
):
    nodes = latent.shape[0]
    gathered, slope, node_sum, node_pre = layer_values(
        latent[...], halo[...], links[...], weights, slope_out.shape[0]
    )
    normed, _ = normalize(node_pre)
    after = (latent[...].astype(F32) + normed * gains[2:3]).astype(BF16)
    latent_out[...] = after
    sent_out[...] = left_transposed(hits(sends[...], nodes), after).astype(BF16)
    gathered_out[...] = gathered
    slope_out[...] = slope.astype(BF16)
    sum_out[...] = node_sum
    node_out[...] = node_pre


def layer_last(
    scale,
    latent,
    halo,
    links,
    weights,
    gains,
    cotangent,
    latent_out,
    gathered_out,
    sum_out,
    norm_out,
    pair_out,
    self_out,
    halo_out,
    up_out,
):
    nodes = latent.shape[0]
    gathered, slope, node_sum, node_pre = layer_values(
        latent[...], halo[...], links[...], weights, links.shape[1] // nodes
    )
    normed, _ = normalize(node_pre)
    latent_out[...] = (latent[...].astype(F32) + normed * gains[3:4]).astype(BF16)
    gathered_out[...] = gathered
    sum_out[...] = node_sum
    upstream = cotangent[...].astype(F32) * scale
    norm_out[...], pair_out[...], self_out[...], halo_out[...], up_out[...] = layer_back(
        upstream, gains[3:4], gathered, slope, node_pre, links[...], weights, halo.shape[0]
    )


def layer_first_back(
    upstream,
    returned,
    sends,
    gathered,
    slope,
    node_pre,
    links,
    weights,
    gains,
    norm_out,
    pair_out,
    self_out,
    halo_out,
    up_out,
):
    nodes = upstream.shape[0]
    total = upstream[...] + matmul(hits(sends[...], nodes), returned[...])
    norm_out[...], pair_out[...], self_out[...], halo_out[...], up_out[...] = layer_back(
        total, gains[2:3], gathered[...], slope[...].astype(F32), node_pre[...], links[...], weights, returned.shape[0]
    )


def weight_grads(core, gathered, grad_pair, latent, grad_self, node_sum, grad_norm, kept, sent):
    blocks, _, rows, width = kept.shape
    pairs = ((gathered, grad_pair), (latent, grad_self), (node_sum, grad_norm))
    for place, (rows_in, grads) in enumerate(pairs):
        total = left_transposed(rows_in[...], grads[...]).reshape(blocks, 2, rows, width)
        first = core[0] == 0
        kept[:, place] = jnp.where(first, total[:, 0], total[:, 1]).astype(BF16)
        sent[:, place] = jnp.where(first, total[:, 1], total[:, 0]).astype(BF16)


def add_cores(chip, kept, other, *outs):
    blocks = kept.shape[0]
    for step, out in enumerate(outs):
        place = lax.rem(chip[0] + step, blocks)
        out[...] = (kept[place].astype(F32) + other[place].astype(F32)).astype(BF16)


def start_back(upstream, returned, sends, mesh_sum, w_node, gains, start_out, sum_out):
    nodes = upstream.shape[0]
    total = upstream[...] + matmul(hits(sends[...], nodes), returned[...])
    normed, inverse = normalize(matmul(mesh_sum[...], w_node[...]))
    grad_start = normalize_back(total * gains[1:2], normed, inverse).astype(BF16)
    start_out[...] = grad_start
    sum_out[...] = right_transposed(grad_start, w_node[...]).astype(BF16)


def edge_back(
    counts,
    core,
    info_west,
    info_own,
    info_east,
    grad_west,
    grad_own,
    grad_east,
    edge_slope,
    edge_rows,
    grid_pre,
    feats,
    sources,
    w_edge,
    gains,
    mesh_sum,
    grad_start,
    kept_out,
    sent_out,
):
    slots = sources.shape[1]
    nodes = grad_own.shape[0]
    channels, grid_nodes = feats.shape
    width = grid_pre.shape[1]
    half = width // 2
    grad_grid = jnp.zeros((grid_nodes, width), F32)
    edge_w = jnp.zeros((width, width), F32)
    sides = ((info_west, grad_west), (info_own, grad_own), (info_east, grad_east))
    for side, (info, grads) in enumerate(sides):
        place = pl.ds(side * slots, slots)
        grad_message = left_transposed(weighted_hits(info[...], nodes), grads[...]).astype(BF16)
        grad_edge = (grad_message.astype(F32) * edge_slope[place].astype(F32)).astype(BF16)
        edge_w += left_transposed(grad_edge, edge_rows[place])
        grad_rows = right_transposed(grad_edge, w_edge[...]).astype(BF16)
        chosen = live_hits(sources[side : side + 1], counts[0, side], grid_nodes)
        grad_grid += matmul(chosen, grad_rows)
    node_w = left_transposed(grad_start[...], mesh_sum[...])
    values = grid_pre[...]
    normed, inverse = normalize(silu(values))
    grad_act = (normalize_back(grad_grid * gains[0:1], normed, inverse) * silu_slope(values)).astype(BF16)
    embed = matmul(feats[...], grad_act)
    spare = 2 * EMBED_HALF - channels
    embed = jnp.concatenate([embed, jnp.zeros((spare, width), F32)], axis=0).T
    low = jnp.concatenate([edge_w[:, :half], node_w[:, :half], embed[:, :EMBED_HALF]], axis=1).astype(BF16)
    high = jnp.concatenate([edge_w[:, half:], node_w[:, half:], embed[:, EMBED_HALF:]], axis=1).astype(BF16)

    @pl.when(core[0] == 0)
    def _():
        kept_out[...] = low
        sent_out[...] = high

    @pl.when(core[0] != 0)
    def _():
        kept_out[...] = high
        sent_out[...] = low


EMBED_HALF = 128


def pack(kept, other, *refs):
    blocks, out = refs[:-1], refs[-1]
    rows = blocks[0].shape[0]
    per = len(blocks) // 2
    for place in range(2):
        total = sum(block[...].astype(F32) for block in blocks[place * per : (place + 1) * per])
        out[:, pl.ds(place * rows, rows)] = total.T.astype(BF16)
    out[:, 2 * rows :] = (kept[...].astype(F32) + other[...].astype(F32)).astype(BF16)


def sum_blocks(blocks, out):
    total = jnp.sum(blocks[...].astype(F32), axis=0).astype(BF16)
    out[...] = jnp.broadcast_to(total[None], out.shape)


def local(
    grid_feats,
    g2m_src,
    g2m_count,
    g2m_dst,
    g2m_weight,
    halo_send,
    mesh_src,
    cotangent,
    w_embed,
    w_encode,
    w_layers,
    gains,
):
    peers = lax.axis_size("mesh")
    bands = lax.axis_size("grid")
    nodes, degree = mesh_src.shape
    grid_nodes, channels = grid_feats.shape
    width = w_embed.shape[1]
    slots = g2m_src.shape[1]
    halo_rows = halo_send.size
    columns = width // peers
    pairs = nodes * degree
    layers = w_layers.shape[0]
    unit = 2 * width * width
    band = lax.axis_index("grid").astype(jnp.int32)
    core = (band % 2).reshape(1)
    chip = (band // 2).reshape(1)
    sends = halo_send.reshape(1, -1)
    links = mesh_src.T.reshape(1, -1)
    feats = grid_feats.T

    edge_info = jnp.stack([g2m_dst.astype(F32), g2m_weight.astype(F32)], axis=1)
    info_west, info_east = from_sides(edge_info[2], edge_info[0])
    info = [info_west, edge_info[1], info_east]
    grid_pre, edge_rows, edge_slope, messages = call(
        edge_forward,
        [
            ((grid_nodes, width), F32),
            ((3 * slots, width), BF16),
            ((3 * slots, width), BF16),
            ((3 * slots, width), BF16),
        ],
        [g2m_count, feats, g2m_src, w_embed, w_encode, gains],
        unit * 8 * slots,
        scalars=(0,),
        picked={4: 0},
    )
    sum_west, sum_own, sum_east = call(
        edge_sums,
        [((nodes, width), BF16), ((nodes, width), F32), ((nodes, width), BF16)],
        [*info, messages],
        unit * slots,
    )
    got_west, got_east = from_sides(sum_east, sum_west)
    mesh_sum, latent, sent = call(
        mesh_start,
        [((nodes, width), BF16), ((nodes, width), BF16), ((halo_rows, width), BF16)],
        [sum_own, got_west, got_east, w_encode, gains, sends],
        unit * nodes * 2,
        picked={3: 1},
    )
    halo = exchange(sent.reshape(peers, -1, width), "mesh").reshape(-1, width)
    gathered, pair_slope, node_sum, node_pre, middle, sent = call(
        layer_forward,
        [
            ((pairs, width), BF16),
            ((degree, nodes, width), BF16),
            ((nodes, width), BF16),
            ((nodes, width), F32),
            ((nodes, width), BF16),
            ((halo_rows, width), BF16),
        ],
        [latent, halo, links, w_layers, gains, sends],
        unit * pairs * 2,
        picked={3: 0},
    )
    halo = exchange(sent.reshape(peers, -1, width), "mesh").reshape(-1, width)
    loss_scale = jnp.full((1,), 1.0 / math.sqrt(nodes * bands * peers), F32)
    back_shapes = [
        ((nodes, width), BF16),
        ((pairs, width), BF16),
        ((nodes, width), BF16),
        ((halo_rows, width), BF16),
        ((nodes, width), F32),
    ]

    def core_halves(*arrays):
        shape = (bands // 2, 3, width // bands, width)
        kept, sent = call(
            weight_grads, [(shape, BF16)] * 2, [core, *arrays], unit * (pairs + 2 * nodes), scalars=(0,)
        )
        rows = (bands // 2, 3 * width // bands, width)
        return call(
            add_cores,
            [(rows[1:], BF16)] * (bands // 2),
            [chip, kept.reshape(rows), to_other_core(sent).reshape(rows)],
            0,
            scalars=(0,),
        )

    def over_chips(parts):
        return [parts[0]] + [along_y(part, step) for step, part in enumerate(parts) if step]

    def last_layer(scale, *refs):
        layer_last(scale[0], *refs)

    mesh_out, last_gathered, last_sum, last_norm, last_pair, last_self, grad_halo, upstream = call(
        last_layer,
        [((nodes, width), BF16), ((pairs, width), BF16), ((nodes, width), BF16)] + back_shapes,
        [loss_scale, middle, halo, links, w_layers, gains, cotangent],
        unit * pairs * 4,
        scalars=(0,),
        picked={4: 1},
    )
    returned = exchange(grad_halo.reshape(peers, -1, width), "mesh").reshape(-1, width)
    last_rows = core_halves(last_gathered, last_pair, middle, last_self, last_sum, last_norm)
    returned, last_rows = lax.optimization_barrier((returned, last_rows))
    last_rows = over_chips(last_rows)
    grad_norm, grad_pair, grad_self, grad_halo, upstream = call(
        layer_first_back,
        back_shapes,
        [upstream, returned, sends, gathered, pair_slope, node_pre, links, w_layers, gains],
        unit * pairs * 3,
        picked={7: 0},
    )
    returned = exchange(grad_halo.reshape(peers, -1, width), "mesh").reshape(-1, width)
    first_rows = core_halves(gathered, grad_pair, latent, grad_self, node_sum, grad_norm)
    chips = bands // 2
    shared = 6 * width // bands
    returned, first_rows = lax.optimization_barrier((returned, first_rows))
    grad_start, grad_sum = call(
        start_back,
        [((nodes, width), BF16), ((nodes, width), BF16)],
        [upstream, returned, sends, mesh_sum, w_encode, gains],
        unit * nodes * 3,
        picked={4: 1},
    )
    grad_west, grad_east = from_sides(grad_sum, grad_sum)
    grad_sum, first_rows, last_rows = lax.optimization_barrier((grad_sum, first_rows, last_rows))
    parts = last_rows + over_chips(first_rows)
    part = width + EMBED_HALF
    kept, passed = call(
        edge_back,
        [((width, part), BF16), ((width, part), BF16)],
        [
            g2m_count,
            core,
            *info,
            grad_west,
            grad_sum,
            grad_east,
            edge_slope,
            edge_rows,
            grid_pre,
            feats,
            g2m_src,
            w_encode,
            gains,
            mesh_sum,
            grad_start,
        ],
        unit * 12 * slots,
        scalars=(0, 1),
        picked={13: 0},
    )
    kept, passed, parts = lax.optimization_barrier((kept, passed, parts))
    other = to_other_core(passed)
    (packed,) = call(
        pack, [((width, shared + part), BF16)], [kept, other, *parts], 0
    )
    arrived = exchange(packed.reshape(peers, columns, -1), "mesh")
    (summed,) = call(sum_blocks, [((bands, columns, shared + part), BF16)], [arrived], 0)
    held = exchange(summed, "grid")
    tail = held[:, :, shared:].reshape(bands // 2, 2, columns, part).astype(F32)
    tail = jnp.sum(tail, axis=0)
    half = width // 2
    embed = jnp.concatenate([tail[0, :, width:], tail[1, :, width:]], axis=1)
    embed = spread(embed.astype(BF16), "mesh")
    total_embed = embed.reshape(width, -1).T[:channels].astype(F32)
    edge_w = jnp.concatenate([tail[0, :, :half], tail[1, :, :half]], axis=1).T
    node_w = jnp.concatenate([tail[0, :, half:width], tail[1, :, half:width]], axis=1).T
    whole = held[:, :, :shared].reshape(bands, columns, layers, 3, width // bands)
    whole = whole[:, :, ::-1].transpose(2, 3, 1, 0, 4).reshape(layers, 3, columns, width).swapaxes(2, 3)
    return mesh_out, whole.astype(F32), jnp.stack([edge_w, node_w]), total_embed


def solution(mesh):
    placed = (P(("grid", "mesh"), None),) * 8 + (P(),) * 4
    return jax.shard_map(
        local,
        mesh=mesh,
        in_specs=placed,
        out_specs=(
            P(("grid", "mesh"), None),
            P(None, None, None, "mesh"),
            P(None, None, "mesh"),
            P(),
        ),
        check_vma=False,
    )
```
